128 devices in a mesh: seq: 16 (over z, x), head: 8 (over y, core).
Axes of the slice: x: 4, y: 4, z: 4, core: 2. Of those that a mesh axis runs over, the one named last changes fastest.
Arguments:
- teacher_query: bfloat16 [2, 4096, 8192], P(None, ('seq', 'head')), may hold values from -6 to 6
- student_query: bfloat16 [2, 4096, 8192], P(None, ('seq', 'head')), may hold values from -6 to 6
- kept_heads: int32 [40], replicated, may hold values from 0 to 63, as said below
Outputs:
- relation_loss: float32 [2, 64, 4096], P(None, 'head', 'seq')
The draws below stay inside these ranges and needn't reach their ends.
Inputs may be any that keep to these rules, and one draw needn't show every extreme that they name: `kept_heads`: the 40 entries are distinct, and 0 and 63 are among them.
All inputs are finite; a program needn't handle non-finite values.
Results may differ from the reference program's by a relative error of at most 0.0003.
Values may be sent and summed in bfloat16 or wider, within the bound.
A program may use at most 128 MiB of HBM per device.

```python
import math
import jax
import jax.numpy as jnp
from jax import lax

HEADS = 64
HD = 128
KEPT = 40
RELH = 64
BATCH = 2
SEQ = 4096
TREL = 128
SREL = 80


def query_rows(key, width):
    key_base = jax.random.fold_in(key, 0)
    base = 0.6 * jnp.clip(jax.random.normal(key_base, (SEQ, width), jnp.float32), -5.0, 5.0)
    return base


def batch_rows(key, width):
    seq_keys = jax.random.split(key, BATCH)
    return jnp.stack([query_rows(seq_keys[index], width) for index in range(BATCH)])


def draw_teacher_query(key, part):
    return batch_rows(jax.random.fold_in(key, 1), HEADS * HD).astype(jnp.bfloat16)


def draw_student_query(key, part):
    return batch_rows(jax.random.fold_in(key, 2), HEADS * HD).astype(jnp.bfloat16)


def draw_kept_heads(key, part):
    key_mid, key_order = jax.random.split(jax.random.fold_in(key, 3))
    middle = jax.random.permutation(key_mid, HEADS - 2)[:KEPT - 2] + 1
    chosen = jnp.concatenate([middle.astype(jnp.int32), jnp.array([0, HEADS - 1], jnp.int32)])
    return jax.random.permutation(key_order, chosen).astype(jnp.int32)


def setup_inputs(seed: int = 0) -> dict:
    splits = jax.random.split(jax.random.key(seed), 4)
    return {
        "teacher_query": draw_teacher_query(jax.random.fold_in(splits[3], 71), 0),
        "student_query": draw_student_query(jax.random.fold_in(splits[3], 71), 0),
        "kept_heads": draw_kept_heads(jax.random.fold_in(splits[3], 71), 0),
    }


NEG_FILL = -1.0e30


def one_sequence(teacher_query, student_query, kept_heads):
    picked = jnp.take(student_query.reshape(SEQ, HEADS, HD), kept_heads, axis=1).reshape(SEQ, KEPT * HD)
    teach_all = jnp.transpose(teacher_query.astype(jnp.float32).reshape(SEQ, RELH, TREL), (1, 0, 2))
    stud_all = jnp.transpose(picked.astype(jnp.float32).reshape(SEQ, RELH, SREL), (1, 0, 2))
    block_rows = math.gcd(SEQ, 512)
    positions = jnp.arange(SEQ, dtype=jnp.int32)

    def per_head(pair):
        teach_head, stud_head = pair

        def per_block(block_number):
            row_start = (block_number * block_rows).astype(jnp.int32)
            query_t = lax.dynamic_slice_in_dim(teach_head, row_start, block_rows, 0)
            query_s = lax.dynamic_slice_in_dim(stud_head, row_start, block_rows, 0)
            teach_scores = jnp.dot(query_t, teach_head.T, precision=lax.Precision.HIGHEST, preferred_element_type=jnp.float32) * (TREL ** -0.5)
            stud_scores = jnp.dot(query_s, stud_head.T, precision=lax.Precision.HIGHEST, preferred_element_type=jnp.float32) * (SREL ** -0.5)
            query_pos = row_start + jnp.arange(block_rows, dtype=jnp.int32)
            allowed = positions[None, :] <= query_pos[:, None]
            teach_scores = jnp.where(allowed, teach_scores, NEG_FILL)
            stud_scores = jnp.where(allowed, stud_scores, NEG_FILL)
            log_t = jax.nn.log_softmax(teach_scores, axis=1)
            log_s = jax.nn.log_softmax(stud_scores, axis=1)
            return jnp.sum(jnp.exp(log_t) * (log_t - log_s), axis=1)

        return lax.map(per_block, jnp.arange(SEQ // block_rows, dtype=jnp.int32)).reshape(SEQ)

    return lax.map(per_head, (teach_all, stud_all))


def reference(teacher_query, student_query, kept_heads):
    def per_sequence(pair):
        return one_sequence(pair[0], pair[1], kept_heads)

    return lax.map(per_sequence, (teacher_query, student_query))
```

```python
import functools
import math

import jax
import jax.numpy as jnp
from jax import lax
from jax.experimental import pallas as pl
from jax.experimental.pallas import tpu as pltpu
from jax.sharding import PartitionSpec as P

HEADS = 64
HD = 128
KEPT = 40
RELH = 64
TREL = 128
SREL = 80

MESH = pl.DeviceIdType.MESH
BF = jnp.bfloat16
F32 = jnp.float32

SCALE_T = math.log2(math.e) / math.sqrt(TREL)
SCALE_S = math.log2(math.e) / math.sqrt(SREL)
OFFSET = 60.0


def params(mesh):
    return mesh.shape["seq"], mesh.shape["head"]


def kernel(
    seq_n, head_n, rows, chunk,
    kept_ref, teach_hbm, stud_hbm, out_ref,
    stud_in, stud_out, tea, stu, tea_shift, stu_query, sums, rows_out, rows_in,
    in_sem, send_t, send_s, recv_t, recv_s, send_o, recv_o,
):
    total = seq_n * head_n
    seq_me = lax.axis_index("seq")
    head_me = lax.axis_index("head")
    me = seq_me * head_n + head_me
    positions = rows * total
    chunks = positions // chunk
    per_chunk = chunk // rows
    my_chunk = me // per_chunk

    def place(t):
        return (t // head_n, lax.rem(t, head_n))

    @pl.loop(0, HEADS)
    def _(i):
        head = stud_hbm.at[:, :, pl.ds(pl.multiple_of(i * HD, HD), HD)]
        pltpu.make_async_copy(head, stud_in.at[i], in_sem).start()

    barrier = pltpu.get_barrier_semaphore()

    @pl.loop(1, total)
    def _(k):
        pl.semaphore_signal(barrier, inc=1, device_id=place(lax.rem(me + k, total)), device_id_type=MESH)

    sums[...] = jnp.zeros_like(sums)
    pltpu.make_async_copy(stud_in, stud_in, in_sem).wait()

    lane = lax.broadcasted_iota(jnp.int32, (rows, HD), 1)

    @pl.loop(0, 2 * head_n)
    def _(bg):
        b = bg // head_n
        g = lax.rem(bg, head_n)
        heads = [stud_in[kept_ref[5 * g + i], b].astype(F32) for i in range(5)]
        for u in range(8):
            first = (u * SREL) // HD
            offset = (u * SREL) % HD
            piece = heads[first]
            if offset:
                piece = pltpu.roll(piece, HD - offset, 1)
            if offset + SREL > HD:
                other = pltpu.roll(heads[first + 1], HD - offset, 1)
                piece = jnp.where(lane < HD - offset, piece, other)
            piece = jnp.where(lane < SREL, piece, jnp.where(lane == SREL, 1.0, 0.0))
            stud_out[(b * 8 + u) * head_n + g] = piece.astype(BF)

    pl.semaphore_wait(barrier, total - 1)

    mine = pl.ds(pl.multiple_of(me * rows, rows), rows)

    def teach_src(t):
        s, h = place(t)
        r = h * 8 + lax.rem(s, 8)
        return teach_hbm.at[s // 8, :, pl.ds(pl.multiple_of(r * TREL, TREL), TREL)]

    own_t = pltpu.make_async_copy(teach_src(me), tea.at[mine], recv_t.at[my_chunk])
    own_s = pltpu.make_async_copy(stud_out.at[me], stu.at[mine], recv_s.at[my_chunk])
    own_t.start()
    own_s.start()

    @pl.loop(1, total)
    def _(k):
        t = lax.rem(me + k, total)
        pltpu.make_async_remote_copy(
            src_ref=teach_src(t), dst_ref=tea.at[mine], send_sem=send_t, recv_sem=recv_t.at[my_chunk],
            device_id=place(t), device_id_type=MESH,
        ).start()
        pltpu.make_async_remote_copy(
            src_ref=stud_out.at[t], dst_ref=stu.at[mine], send_sem=send_s, recv_sem=recv_s.at[my_chunk],
            device_id=place(t), device_id_type=MESH,
        ).start()

    half = chunk // 2
    row_i = lax.broadcasted_iota(jnp.int32, (TREL, HD), 0)
    col_i = lax.broadcasted_iota(jnp.int32, (TREL, HD), 1)
    pick_t = jnp.where(col_i == 0, 1.0, 0.0).astype(BF)
    pick_s = jnp.where((col_i == SREL) & (row_i < SREL), 1.0, 0.0).astype(BF)
    chunk_lane = lax.broadcasted_iota(jnp.int32, (chunk, HD), 1)
    ones_t = jnp.where(chunk_lane == 0, 1.0, 0.0).astype(BF)

    def rows_dot(x, y):
        return lax.dot_general(x, y, (((1,), (1,)), ((), ())), preferred_element_type=F32)

    def tile(key_start, key_count, query_start, masked):
        keys = pl.ds(pl.multiple_of(key_start, half), key_count)
        queries = pl.ds(pl.multiple_of(query_start, half), half)
        key_t = jnp.concatenate([tea[keys], ones_t[:key_count]], axis=1)
        key_s = stu[keys]
        key_s = jnp.concatenate([key_s, key_s], axis=1)
        query_t = jnp.concatenate([tea[queries], tea_shift[queries]], axis=1)
        query_s = stu_query[queries]
        score_t = rows_dot(key_t, query_t) * SCALE_T
        score_s = rows_dot(key_s, query_s)
        if masked:
            key_i = lax.broadcasted_iota(jnp.int32, (key_count, half), 0)
            query_i = lax.broadcasted_iota(jnp.int32, (key_count, half), 1)
            seen = key_i <= query_i + (key_count - half)
            score_t = jnp.where(seen, score_t, -1e30)
            score_s = jnp.where(seen, score_s, -1e30)
        weight_t = jnp.exp2(score_t)
        weight_s = jnp.exp2(score_s)
        cross = weight_t * (score_t - score_s)
        fold = lambda x: jnp.sum(x.reshape(key_count // 8, 8, half), axis=0)
        sums[0, :, queries] += fold(weight_t)
        sums[1, :, queries] += fold(weight_s)
        sums[2, :, queries] += fold(cross)

    @pl.loop(1, chunks + 1)
    def _(n):
        c = lax.rem(my_chunk - n + chunks, chunks)
        here = pl.ds(pl.multiple_of(c * chunk, chunk), chunk)
        pltpu.make_async_copy(tea.at[here], tea.at[here], recv_t.at[c]).wait()
        pltpu.make_async_copy(stu.at[here], stu.at[here], recv_s.at[c]).wait()

        a = tea[here].astype(F32)
        norm_t = jnp.dot((a * a).astype(BF), pick_t, preferred_element_type=F32)
        tea_shift[here] = jnp.where(chunk_lane == 0, -OFFSET / SCALE_T - norm_t, 0.0).astype(BF)
        b = stu[here].astype(F32)
        norm_s = jnp.dot((b * b).astype(BF), pick_s, preferred_element_type=F32)
        scaled = jnp.where(chunk_lane < SREL, b * SCALE_S, 0.0)
        high = scaled.astype(BF)
        low = (scaled - high.astype(F32)).astype(BF)
        high = jnp.where(chunk_lane == SREL, -OFFSET - SCALE_S * norm_s, high.astype(F32)).astype(BF)
        stu_query[here] = jnp.concatenate([high, low], axis=1)

        @pl.loop(1, n)
        def _(m):
            d = lax.rem(my_chunk - m + chunks, chunks)
            upper, lower = jnp.maximum(c, d), jnp.minimum(c, d)
            tile(lower * chunk, chunk, upper * chunk, False)
            tile(lower * chunk, chunk, upper * chunk + half, False)

        tile(c * chunk, half, c * chunk, True)
        tile(c * chunk, chunk, c * chunk + half, True)

    each = positions // seq_n
    for j in range(seq_n):
        part = pl.ds(j * each, each)
        total_t = jnp.sum(sums[0, :, part], axis=0, keepdims=True)
        total_s = jnp.sum(sums[1, :, part], axis=0, keepdims=True)
        cross = jnp.sum(sums[2, :, part], axis=0, keepdims=True)
        rows_out[j] = (cross / total_t - jnp.log2(total_t) + jnp.log2(total_s)) * math.log(2.0)

    own_o = pltpu.make_async_copy(rows_out.at[seq_me], rows_in.at[seq_me], recv_o)
    own_o.start()

    @pl.loop(1, seq_n)
    def _(k):
        s = lax.rem(seq_me + k, seq_n)
        pltpu.make_async_remote_copy(
            src_ref=rows_out.at[s], dst_ref=rows_in.at[seq_me], send_sem=send_o, recv_sem=recv_o,
            device_id=(s, head_me), device_id_type=MESH,
        ).start()

    pltpu.make_async_copy(rows_in, rows_in, recv_o).wait()
    out_ref[...] = rows_in[...].reshape(2, 8, each)

    sent = pl.ds(0, (total - 1) * rows)
    pltpu.make_async_copy(tea.at[sent], tea.at[sent], send_t).wait()
    pltpu.make_async_copy(stu.at[sent], stu.at[sent], send_s).wait()
    others = pl.ds(0, seq_n - 1)
    pltpu.make_async_copy(rows_in.at[others], rows_in.at[others], send_o).wait()


def shards(seq_n, head_n, teacher_query, student_query, kept_heads):
    batch, rows, width = teacher_query.shape
    total = seq_n * head_n
    positions = rows * total
    chunk = 512
    chunks = positions // chunk
    each = positions // seq_n
    vm = pltpu.VMEM
    dma = pltpu.SemaphoreType.DMA
    return pl.pallas_call(
        functools.partial(kernel, seq_n, head_n, rows, chunk),
        out_shape=jax.ShapeDtypeStruct((batch, RELH // head_n, each), F32),
        in_specs=[
            pl.BlockSpec(memory_space=pltpu.SMEM),
            pl.BlockSpec(memory_space=pl.ANY),
            pl.BlockSpec(memory_space=pl.ANY),
        ],
        out_specs=pl.BlockSpec(memory_space=pltpu.VMEM),
        scratch_shapes=[
            vm((HEADS, batch, rows, HD), BF),
            vm((total, rows, HD), BF),
            vm((positions, TREL), BF),
            vm((positions, HD), BF),
            vm((positions, HD), BF),
            vm((positions, 2 * HD), BF),
            vm((3, 8, positions), F32),
            vm((seq_n, 1, each), F32),
            vm((seq_n, 1, each), F32),
            dma, dma, dma, dma((chunks,)), dma((chunks,)), dma, dma,
        ],
        compiler_params=pltpu.CompilerParams(
            collective_id=0, has_side_effects=True, vmem_limit_bytes=48 * 2**20
        ),
    )(kept_heads, teacher_query, student_query)


def solution(mesh):
    seq_n, head_n = params(mesh)
    placed = (P(None, ("seq", "head"), None), P(None, ("seq", "head"), None), P())
    return jax.shard_map(
        functools.partial(shards, seq_n, head_n),
        mesh=mesh, in_specs=placed, out_specs=P(None, "head", "seq"), check_vma=False,
    )
```

```python
import functools
import math

import jax
import jax.numpy as jnp
from jax import lax
from jax.experimental import pallas as pl
from jax.experimental.pallas import tpu as pltpu
from jax.sharding import PartitionSpec as P

HEADS = 64
HD = 128
KEPT = 40
RELH = 64
TREL = 128
SREL = 80

MESH = pl.DeviceIdType.MESH
BF = jnp.bfloat16
F32 = jnp.float32

SCALE_T = math.log2(math.e) / math.sqrt(TREL)
SCALE_S = math.log2(math.e) / math.sqrt(SREL)
OFFSET = 60.0


def params(mesh):
    return mesh.shape["seq"], mesh.shape["head"]


ORDER = (1, 3, 2, 0)
AHEAD = 4


def xor2(a, b):
    bits = [lax.rem(lax.div(a, w) + lax.div(b, w), 2) * w for w in (1, 2)]
    return bits[0] + bits[1]


def kernel(
    seq_n, head_n, rows, chunk,
    kept_ref, teach_hbm, stud_hbm, out_ref,
    teach_in, stud_in, stud_out, packed, tea, stu, tea_shift, stu_query, sums, rows_out, rows_in,
    in_t, in_sem, send_t, send_s, recv_t, recv_s, send_o, recv_o,
):
    total = seq_n * head_n
    seq_me = lax.axis_index("seq")
    head_me = lax.axis_index("head")
    me = seq_me * head_n + head_me
    positions = rows * total
    chunks = positions // chunk
    per_chunk = chunk // rows
    my_chunk = lax.div(seq_me, 4)
    core_me = lax.rem(head_me, 2)
    y_me = lax.div(head_me, 2)
    x_me = lax.rem(seq_me, 4)

    def chunk_at(step, core):
        code = jnp.int32(ORDER[0])
        for i in range(1, chunks):
            code = jnp.where(step == i, ORDER[i], code)
        return xor2(xor2(my_chunk, code), 2 * core)

    barrier = pltpu.get_barrier_semaphore()

    heads_from_me = [lax.rem(head_me + i, head_n) for i in range(head_n)]
    for h in heads_from_me[1:]:
        pl.semaphore_signal(barrier, inc=1, device_id=(seq_me, h), device_id_type=MESH)

    @pl.loop(1, seq_n)
    def _(k):
        s = lax.rem(seq_me + k, seq_n)
        for h in heads_from_me:
            pl.semaphore_signal(barrier, inc=1, device_id=(s, h), device_id_type=MESH)

    @pl.loop(0, HEADS)
    def _(i):
        head = stud_hbm.at[:, :, pl.ds(pl.multiple_of(i * HD, HD), HD)]
        pltpu.make_async_copy(head, stud_in.at[i], in_sem).start()

    load_t = pltpu.make_async_copy(teach_hbm, teach_in, in_t)
    load_t.start()

    sums[...] = jnp.zeros_like(sums)
    pltpu.make_async_copy(stud_in, stud_in, in_sem).wait()

    lane = lax.broadcasted_iota(jnp.int32, (rows, HD), 1)
    tile_lane = lax.broadcasted_iota(jnp.int32, (8, HD), 1)

    @pl.loop(0, 2 * head_n)
    def _(bg):
        b = lax.div(bg, head_n)
        g = lax.rem(bg, head_n)
        heads = [stud_in[kept_ref[5 * g + i], b].astype(F32) for i in range(5)]
        for u in range(8):
            first = (u * SREL) // HD
            offset = (u * SREL) % HD
            piece = heads[first]
            if offset:
                piece = pltpu.roll(piece, HD - offset, 1)
            if offset + SREL > HD:
                other = pltpu.roll(heads[first + 1], HD - offset, 1)
                piece = jnp.where(lane < HD - offset, piece, other)
            v = piece.reshape(4, 8, HD)
            rest = [pltpu.roll(v[i], 64 + 16 * i, 1) for i in range(4)]
            rest = jnp.where(tile_lane < 32, jnp.where(tile_lane < 16, rest[0], rest[1]), jnp.where(tile_lane < 48, rest[2], rest[3]))
            to = (b * 8 + u) * head_n + g
            stud_out[to, 0] = jnp.where(tile_lane < 64, v[0], pltpu.roll(v[2], 64, 1)).astype(BF)
            stud_out[to, 1] = jnp.where(tile_lane < 64, v[1], pltpu.roll(v[3], 64, 1)).astype(BF)
            stud_out[to, 2] = rest.astype(BF)

    load_t.wait()
    pl.semaphore_wait(barrier, total - 1)

    mine = pl.ds(pl.multiple_of(me * rows, rows), rows)

    def teach_src(s, h):
        r = h * 8 + lax.rem(s, 8)
        return teach_in.at[lax.div(s, 8), :, pl.ds(pl.multiple_of(r * TREL, TREL), TREL)]

    own_t = pltpu.make_async_copy(teach_src(seq_me, head_me), tea.at[mine], recv_t.at[my_chunk])
    own_s = pltpu.make_async_copy(stud_out.at[me], packed.at[me], recv_s.at[my_chunk])
    own_t.start()
    own_s.start()

    x_at = [lax.rem(x_me + i, 4) for i in range(4)]
    y_at = [lax.rem(y_me + i, 4) for i in range(4)]

    def send(step):
        chunk_of = [chunk_at(step, core) for core in range(2)]
        for j in range(per_chunk):
            core, x = j % 2, (j // 2) % 4
            y = (x + j // 8) % 4
            s = chunk_of[core] * 4 + x_at[x]
            h = y_at[y] * 2 + core

            def copies(s=s, h=h):
                pltpu.make_async_remote_copy(
                    src_ref=teach_src(s, h), dst_ref=tea.at[mine], send_sem=send_t, recv_sem=recv_t.at[my_chunk],
                    device_id=(s, h), device_id_type=MESH,
                ).start()
                pltpu.make_async_remote_copy(
                    src_ref=stud_out.at[s * head_n + h], dst_ref=packed.at[me], send_sem=send_s,
                    recv_sem=recv_s.at[my_chunk], device_id=(s, h), device_id_type=MESH,
                ).start()

            if x == 0 and y == 0:
                pl.when((s != seq_me) | (h != head_me))(copies)
            else:
                copies()

    @pl.loop(0, AHEAD)
    def _(step):
        send(step)

    part = 256
    row_i = lax.broadcasted_iota(jnp.int32, (TREL, HD), 0)
    col_i = lax.broadcasted_iota(jnp.int32, (TREL, HD), 1)
    pick_t = jnp.where(col_i == 0, 1.0, 0.0).astype(BF)
    pick_s = jnp.where((col_i == SREL) & (row_i < SREL), 1.0, 0.0).astype(BF)
    chunk_lane = lax.broadcasted_iota(jnp.int32, (chunk, HD), 1)
    ones_t = jnp.where(chunk_lane == 0, 1.0, 0.0).astype(BF)

    def rows_dot(x, y):
        return lax.dot_general(x, y, (((1,), (1,)), ((), ())), preferred_element_type=F32)

    def scores(key_start, key_count, query_start):
        keys = pl.ds(pl.multiple_of(key_start, part), key_count)
        queries = pl.ds(pl.multiple_of(query_start, part), part)
        key_t = jnp.concatenate([tea[keys], ones_t[:key_count]], axis=1)
        key_s = stu[keys]
        key_s = jnp.concatenate([key_s, key_s], axis=1)
        query_t = jnp.concatenate([tea[queries], tea_shift[queries]], axis=1)
        return rows_dot(key_t, query_t) * SCALE_T, rows_dot(key_s, stu_query[queries])

    def add(query_start, pairs):
        queries = pl.ds(pl.multiple_of(query_start, part), part)
        fold = lambda x: jnp.sum(x.reshape(-1, 8, part), axis=0)
        for score_t, score_s in pairs:
            weight_t = jnp.exp2(score_t)
            weight_s = jnp.exp2(score_s)
            sums[0, :, queries] += fold(weight_t)
            sums[1, :, queries] += fold(weight_s)
            sums[2, :, queries] += fold(weight_t * (score_t - score_s))

    def below(key_start, query_start):
        for q in range(0, chunk, part):
            add(query_start + q, [scores(key_start, chunk, query_start + q)])

    def diagonal(start):
        key_i = lax.broadcasted_iota(jnp.int32, (part, part), 0)
        query_i = lax.broadcasted_iota(jnp.int32, (part, part), 1)
        seen = key_i <= query_i
        for q in range(0, chunk, part):
            score_t, score_s = scores(start, q + part, start + q)
            pairs = [(jnp.where(seen, score_t[q:], -1e30), jnp.where(seen, score_s[q:], -1e30))]
            if q:
                pairs.append((score_t[:q], score_s[:q]))
            add(start + q, pairs)

    @pl.loop(0, chunks)
    def _(n):
        c = chunk_at(n, core_me)
        here = pl.ds(pl.multiple_of(c * chunk, chunk), chunk)
        pltpu.make_async_copy(tea.at[here], tea.at[here], recv_t.at[c]).wait()
        from_c = pl.ds(pl.multiple_of(c * per_chunk, per_chunk), per_chunk)
        pltpu.make_async_copy(packed.at[from_c], packed.at[from_c], recv_s.at[c]).wait()

        @pl.when(n + AHEAD < chunks)
        def _():
            send(n + AHEAD)

        a = tea[here].astype(F32)
        norm_t = jnp.dot((a * a).astype(BF), pick_t, preferred_element_type=F32)
        tea_shift[here] = jnp.where(chunk_lane == 0, -OFFSET / SCALE_T - norm_t, 0.0).astype(BF)
        u = packed[from_c].astype(F32)
        lanes = lax.broadcasted_iota(jnp.int32, (per_chunk, 8, HD), 2)
        first = [u[:, 0], u[:, 1], pltpu.roll(u[:, 0], 64, 2), pltpu.roll(u[:, 1], 64, 2)]
        b = jnp.stack(
            [jnp.where(lanes < 64, first[i], pltpu.roll(u[:, 2], 64 - 16 * i, 2)) for i in range(4)], axis=1
        ).reshape(chunk, HD)
        b = jnp.where(chunk_lane < SREL, b, 0.0)
        stu[here] = jnp.where(chunk_lane == SREL, 1.0, b).astype(BF)
        norm_s = jnp.dot((b * b).astype(BF), pick_s, preferred_element_type=F32)
        scaled = b * SCALE_S
        high = scaled.astype(BF)
        low = (scaled - high.astype(F32)).astype(BF)
        high = jnp.where(chunk_lane == SREL, -OFFSET - SCALE_S * norm_s, high.astype(F32)).astype(BF)
        stu_query[here] = jnp.concatenate([high, low], axis=1)

        @pl.loop(0, n)
        def _(m):
            d = chunk_at(m, core_me)
            upper, lower = jnp.maximum(c, d), jnp.minimum(c, d)
            below(lower * chunk, upper * chunk)

        diagonal(c * chunk)

    each = positions // seq_n
    for j in range(seq_n):
        part = pl.ds(j * each, each)
        total_t = jnp.sum(sums[0, :, part], axis=0, keepdims=True)
        total_s = jnp.sum(sums[1, :, part], axis=0, keepdims=True)
        cross = jnp.sum(sums[2, :, part], axis=0, keepdims=True)
        rows_out[j] = (cross / total_t - jnp.log2(total_t) + jnp.log2(total_s)) * math.log(2.0)

    own_o = pltpu.make_async_copy(rows_out.at[seq_me], rows_in.at[seq_me], recv_o)
    own_o.start()

    @pl.loop(1, seq_n)
    def _(k):
        s = lax.rem(seq_me + k, seq_n)
        pltpu.make_async_remote_copy(
            src_ref=rows_out.at[s], dst_ref=rows_in.at[seq_me], send_sem=send_o, recv_sem=recv_o,
            device_id=(s, head_me), device_id_type=MESH,
        ).start()

    pltpu.make_async_copy(rows_in, rows_in, recv_o).wait()
    out_ref[...] = rows_in[...].reshape(2, 8, each)

    sent = pl.ds(0, (total - 1) * rows)
    sent_s = pl.ds(0, total - 1)
    pltpu.make_async_copy(tea.at[sent], tea.at[sent], send_t).wait()
    pltpu.make_async_copy(packed.at[sent_s], packed.at[sent_s], send_s).wait()
    others = pl.ds(0, seq_n - 1)
    pltpu.make_async_copy(rows_in.at[others], rows_in.at[others], send_o).wait()


def shards(seq_n, head_n, teacher_query, student_query, kept_heads):
    batch, rows, width = teacher_query.shape
    total = seq_n * head_n
    positions = rows * total
    chunk = 1024
    chunks = positions // chunk
    each = positions // seq_n
    vm = pltpu.VMEM
    dma = pltpu.SemaphoreType.DMA
    return pl.pallas_call(
        functools.partial(kernel, seq_n, head_n, rows, chunk),
        out_shape=jax.ShapeDtypeStruct((batch, RELH // head_n, each), F32),
        in_specs=[
            pl.BlockSpec(memory_space=pltpu.SMEM),
            pl.BlockSpec(memory_space=pltpu.HBM),
            pl.BlockSpec(memory_space=pltpu.HBM),
        ],
        out_specs=pl.BlockSpec(memory_space=pltpu.VMEM),
        scratch_shapes=[
            vm((batch, rows, width), BF),
            vm((HEADS, batch, rows, HD), BF),
            vm((total, 3, 8, HD), BF),
            vm((total, 3, 8, HD), BF),
            vm((positions, TREL), BF),
            vm((positions, HD), BF),
            vm((positions, HD), BF),
            vm((positions, 2 * HD), BF),
            vm((3, 8, positions), F32),
            vm((seq_n, 1, each), F32),
            vm((seq_n, 1, each), F32),
            dma, dma, dma, dma, dma((chunks,)), dma((chunks,)), dma, dma,
        ],
        compiler_params=pltpu.CompilerParams(
            collective_id=0, has_side_effects=True, vmem_limit_bytes=48 * 2**20
        ),
    )(kept_heads, teacher_query, student_query)


def solution(mesh):
    seq_n, head_n = params(mesh)
    placed = (P(None, ("seq", "head"), None), P(None, ("seq", "head"), None), P())
    return jax.shard_map(
        functools.partial(shards, seq_n, head_n),
        mesh=mesh, in_specs=placed, out_specs=P(None, "head", "seq"), check_vma=False,
    )
```

```python
import functools
import math

import jax
import jax.numpy as jnp
from jax import lax
from jax.experimental import pallas as pl
from jax.experimental.pallas import tpu as pltpu
from jax.sharding import PartitionSpec as P

HEADS = 64
HD = 128
KEPT = 40
RELH = 64
TREL = 128
SREL = 80

MESH = pl.DeviceIdType.MESH
BF = jnp.bfloat16
F32 = jnp.float32

SCALE_T = math.log2(math.e) / math.sqrt(TREL)
SCALE_S = math.log2(math.e) / math.sqrt(SREL)
OFFSET = 60.0


def params(mesh):
    return mesh.shape["seq"], mesh.shape["head"]


ORDER = (1, 3, 2, 0)
AHEAD = 4


def xor2(a, b):
    bits = [lax.rem(lax.div(a, w) + lax.div(b, w), 2) * w for w in (1, 2)]
    return bits[0] + bits[1]


def kernel(
    seq_n, head_n, rows, chunk,
    kept_ref, teach_hbm, stud_hbm, out_ref,
    teach_in, stud_in, stud_out, packed, tea, stu, tea_shift, stu_query, sums, rows_out, rows_in,
    in_t, in_sem, send_t, send_s, recv_t, recv_s, send_o, recv_o,
):
    total = seq_n * head_n
    seq_me = lax.axis_index("seq")
    head_me = lax.axis_index("head")
    me = seq_me * head_n + head_me
    positions = rows * total
    chunks = positions // chunk
    per_chunk = chunk // rows
    my_chunk = lax.div(seq_me, 4)
    core_me = lax.rem(head_me, 2)
    y_me = lax.div(head_me, 2)
    x_me = lax.rem(seq_me, 4)

    def chunk_at(step, core):
        code = jnp.int32(ORDER[0])
        for i in range(1, chunks):
            code = jnp.where(step == i, ORDER[i], code)
        return xor2(xor2(my_chunk, code), 2 * core)

    barrier = pltpu.get_barrier_semaphore()

    heads_from_me = [lax.rem(head_me + i, head_n) for i in range(head_n)]
    for h in heads_from_me[1:]:
        pl.semaphore_signal(barrier, inc=1, device_id=(seq_me, h), device_id_type=MESH)

    @pl.loop(1, seq_n)
    def _(k):
        s = lax.rem(seq_me + k, seq_n)
        for h in heads_from_me:
            pl.semaphore_signal(barrier, inc=1, device_id=(s, h), device_id_type=MESH)

    @pl.loop(0, HEADS)
    def _(i):
        head = stud_hbm.at[:, :, pl.ds(pl.multiple_of(i * HD, HD), HD)]
        pltpu.make_async_copy(head, stud_in.at[i], in_sem).start()

    load_t = pltpu.make_async_copy(teach_hbm, teach_in, in_t)
    load_t.start()

    sums[...] = jnp.zeros_like(sums)
    pltpu.make_async_copy(stud_in, stud_in, in_sem).wait()

    lane = lax.broadcasted_iota(jnp.int32, (rows, HD), 1)
    tile_lane = lax.broadcasted_iota(jnp.int32, (8, HD), 1)

    @pl.loop(0, 2 * head_n)
    def _(bg):
        b = lax.div(bg, head_n)
        g = lax.rem(bg, head_n)
        heads = [stud_in[kept_ref[5 * g + i], b].astype(F32) for i in range(5)]
        for u in range(8):
            first = (u * SREL) // HD
            offset = (u * SREL) % HD
            piece = heads[first]
            if offset:
                piece = pltpu.roll(piece, HD - offset, 1)
            if offset + SREL > HD:
                other = pltpu.roll(heads[first + 1], HD - offset, 1)
                piece = jnp.where(lane < HD - offset, piece, other)
            v = piece.reshape(4, 8, HD)
            rest = [pltpu.roll(v[i], 64 + 16 * i, 1) for i in range(4)]
            rest = jnp.where(tile_lane < 32, jnp.where(tile_lane < 16, rest[0], rest[1]), jnp.where(tile_lane < 48, rest[2], rest[3]))
            to = (b * 8 + u) * head_n + g
            stud_out[to, 0] = jnp.where(tile_lane < 64, v[0], pltpu.roll(v[2], 64, 1)).astype(BF)
            stud_out[to, 1] = jnp.where(tile_lane < 64, v[1], pltpu.roll(v[3], 64, 1)).astype(BF)
            stud_out[to, 2] = rest.astype(BF)

    load_t.wait()
    pl.semaphore_wait(barrier, total - 1)

    mine = pl.ds(pl.multiple_of(me * rows, rows), rows)

    def teach_src(s, h):
        r = h * 8 + lax.rem(s, 8)
        return teach_in.at[lax.div(s, 8), :, pl.ds(pl.multiple_of(r * TREL, TREL), TREL)]

    own_t = pltpu.make_async_copy(teach_src(seq_me, head_me), tea.at[mine], recv_t.at[my_chunk])
    own_s = pltpu.make_async_copy(stud_out.at[me], packed.at[me], recv_s.at[my_chunk])
    own_t.start()
    own_s.start()

    x_at = [lax.rem(x_me + i, 4) for i in range(4)]
    y_at = [lax.rem(y_me + i, 4) for i in range(4)]

    def send(step):
        chunk_of = [chunk_at(step, core) for core in range(2)]
        for j in range(per_chunk):
            core, x = j % 2, (j // 2) % 4
            y = (x + j // 8) % 4
            s = chunk_of[core] * 4 + x_at[x]
            h = y_at[y] * 2 + core

            def copies(s=s, h=h):
                pltpu.make_async_remote_copy(
                    src_ref=teach_src(s, h), dst_ref=tea.at[mine], send_sem=send_t, recv_sem=recv_t.at[my_chunk],
                    device_id=(s, h), device_id_type=MESH,
                ).start()
                pltpu.make_async_remote_copy(
                    src_ref=stud_out.at[s * head_n + h], dst_ref=packed.at[me], send_sem=send_s,
                    recv_sem=recv_s.at[my_chunk], device_id=(s, h), device_id_type=MESH,
                ).start()

            if x == 0 and y == 0:
                pl.when((s != seq_me) | (h != head_me))(copies)
            else:
                copies()

    @pl.loop(0, AHEAD)
    def _(step):
        send(step)

    part = 256
    row_i = lax.broadcasted_iota(jnp.int32, (TREL, HD), 0)
    col_i = lax.broadcasted_iota(jnp.int32, (TREL, HD), 1)
    pick_t = jnp.where(col_i == 0, 1.0, 0.0).astype(BF)
    pick_s = jnp.where((col_i == SREL) & (row_i < SREL), 1.0, 0.0).astype(BF)
    chunk_lane = lax.broadcasted_iota(jnp.int32, (chunk, HD), 1)
    ones_t = jnp.where(chunk_lane == 0, 1.0, 0.0).astype(BF)

    def rows_dot(x, y):
        return lax.dot_general(x, y, (((1,), (1,)), ((), ())), preferred_element_type=F32)

    def scores(key_start, key_count, query_start):
        keys = pl.ds(pl.multiple_of(key_start, part), key_count)
        queries = pl.ds(pl.multiple_of(query_start, part), part)
        key_t = jnp.concatenate([tea[keys], ones_t[:key_count]], axis=1)
        key_s = stu[keys]
        key_s = jnp.concatenate([key_s, key_s], axis=1)
        query_t = jnp.concatenate([tea[queries], tea_shift[queries]], axis=1)
        return rows_dot(key_t, query_t) * SCALE_T, rows_dot(key_s, stu_query[queries])

    def add(query_start, pairs):
        queries = pl.ds(pl.multiple_of(query_start, part), part)
        fold = lambda x: jnp.sum(x.reshape(-1, 8, part), axis=0)
        for score_t, score_s in pairs:
            weight_t = jnp.exp2(score_t)
            weight_s = jnp.exp2(score_s)
            sums[0, :, queries] += fold(weight_t)
            sums[1, :, queries] += fold(weight_s)
            sums[2, :, queries] += fold(weight_t * (score_t - score_s))

    def below(key_start, query_start):
        for q in range(0, chunk, part):
            add(query_start + q, [scores(key_start, chunk, query_start + q)])

    def diagonal(start):
        key_i = lax.broadcasted_iota(jnp.int32, (part, part), 0)
        query_i = lax.broadcasted_iota(jnp.int32, (part, part), 1)
        seen = key_i <= query_i
        for q in range(0, chunk, part):
            score_t, score_s = scores(start, q + part, start + q)
            pairs = [(jnp.where(seen, score_t[q:], -1e30), jnp.where(seen, score_s[q:], -1e30))]
            if q:
                pairs.append((score_t[:q], score_s[:q]))
            add(start + q, pairs)

    @pl.loop(0, chunks)
    def _(n):
        c = chunk_at(n, core_me)
        here = pl.ds(pl.multiple_of(c * chunk, chunk), chunk)
        pltpu.make_async_copy(tea.at[here], tea.at[here], recv_t.at[c]).wait()
        from_c = pl.ds(pl.multiple_of(c * per_chunk, per_chunk), per_chunk)
        pltpu.make_async_copy(packed.at[from_c], packed.at[from_c], recv_s.at[c]).wait()

        @pl.when(n + AHEAD < chunks)
        def _():
            send(n + AHEAD)

        a = tea[here].astype(F32)
        norm_t = jnp.dot((a * a).astype(BF), pick_t, preferred_element_type=F32)
        tea_shift[here] = jnp.where(chunk_lane == 0, -OFFSET / SCALE_T - norm_t, 0.0).astype(BF)
        u = packed[from_c].astype(F32)
        lanes = lax.broadcasted_iota(jnp.int32, (per_chunk, 8, HD), 2)
        first = [u[:, 0], u[:, 1], pltpu.roll(u[:, 0], 64, 2), pltpu.roll(u[:, 1], 64, 2)]
        b = jnp.stack(
            [jnp.where(lanes < 64, first[i], pltpu.roll(u[:, 2], 64 - 16 * i, 2)) for i in range(4)], axis=1
        ).reshape(chunk, HD)
        b = jnp.where(chunk_lane < SREL, b, 0.0)
        stu[here] = jnp.where(chunk_lane == SREL, 1.0, b).astype(BF)
        norm_s = jnp.dot((b * b).astype(BF), pick_s, preferred_element_type=F32)
        scaled = b * SCALE_S
        high = scaled.astype(BF)
        low = (scaled - high.astype(F32)).astype(BF)
        high = jnp.where(chunk_lane == SREL, -OFFSET - SCALE_S * norm_s, high.astype(F32)).astype(BF)
        stu_query[here] = jnp.concatenate([high, low], axis=1)

        @pl.loop(0, n)
        def _(m):
            d = chunk_at(m, core_me)
            upper, lower = jnp.maximum(c, d), jnp.minimum(c, d)
            below(lower * chunk, upper * chunk)

        diagonal(c * chunk)

    each = positions // seq_n
    for j in range(seq_n):
        part = pl.ds(j * each, each)
        total_t = jnp.sum(sums[0, :, part], axis=0, keepdims=True)
        total_s = jnp.sum(sums[1, :, part], axis=0, keepdims=True)
        cross = jnp.sum(sums[2, :, part], axis=0, keepdims=True)
        rows_out[j] = (cross / total_t - jnp.log2(total_t) + jnp.log2(total_s)) * math.log(2.0)

    own_o = pltpu.make_async_copy(rows_out.at[seq_me], rows_in.at[seq_me], recv_o)
    own_o.start()

    @pl.loop(1, seq_n)
    def _(k):
        s = lax.rem(seq_me + k, seq_n)
        pltpu.make_async_remote_copy(
            src_ref=rows_out.at[s], dst_ref=rows_in.at[seq_me], send_sem=send_o, recv_sem=recv_o,
            device_id=(s, head_me), device_id_type=MESH,
        ).start()

    pltpu.make_async_copy(rows_in, rows_in, recv_o).wait()
    out_ref[...] = rows_in[...].reshape(2, 8, each)

    sent = pl.ds(0, (total - 1) * rows)
    sent_s = pl.ds(0, total - 1)
    pltpu.make_async_copy(tea.at[sent], tea.at[sent], send_t).wait()
    pltpu.make_async_copy(packed.at[sent_s], packed.at[sent_s], send_s).wait()
    others = pl.ds(0, seq_n - 1)
    pltpu.make_async_copy(rows_in.at[others], rows_in.at[others], send_o).wait()


def shards(seq_n, head_n, teacher_query, student_query, kept_heads):
    batch, rows, width = teacher_query.shape
    total = seq_n * head_n
    positions = rows * total
    chunk = 1024
    chunks = positions // chunk
    each = positions // seq_n
    vm = pltpu.VMEM
    dma = pltpu.SemaphoreType.DMA
    return pl.pallas_call(
        functools.partial(kernel, seq_n, head_n, rows, chunk),
        out_shape=jax.ShapeDtypeStruct((batch, RELH // head_n, each), F32),
        in_specs=[
            pl.BlockSpec(memory_space=pltpu.SMEM),
            pl.BlockSpec(memory_space=pltpu.HBM),
            pl.BlockSpec(memory_space=pltpu.HBM),
        ],
        out_specs=pl.BlockSpec(memory_space=pltpu.VMEM),
        scratch_shapes=[
            vm((batch, rows, width), BF),
            vm((HEADS, batch, rows, HD), BF),
            vm((total, 3, 8, HD), BF),
            vm((total, 3, 8, HD), BF),
            vm((positions, TREL), BF),
            vm((positions, HD), BF),
            vm((positions, HD), BF),
            vm((positions, 2 * HD), BF),
            vm((3, 8, positions), F32),
            vm((seq_n, 1, each), F32),
            vm((seq_n, 1, each), F32),
            dma, dma, dma, dma, dma((chunks,)), dma((chunks,)), dma, dma,
        ],
        compiler_params=pltpu.CompilerParams(
            collective_id=0, has_side_effects=True, vmem_limit_bytes=60 * 2**20
        ),
    )(kept_heads, teacher_query, student_query)


def solution(mesh):
    seq_n, head_n = params(mesh)
    placed = (P(None, ("seq", "head"), None), P(None, ("seq", "head"), None), P())
    return jax.shard_map(
        functools.partial(shards, seq_n, head_n),
        mesh=mesh, in_specs=placed, out_specs=P(None, "head", "seq"), check_vma=False,
    )
```

```python
import functools
import math

import jax
import jax.numpy as jnp
from jax import lax
from jax.experimental import pallas as pl
from jax.experimental.pallas import tpu as pltpu
from jax.sharding import PartitionSpec as P

HEADS = 64
HD = 128
KEPT = 40
RELH = 64
TREL = 128
SREL = 80

MESH = pl.DeviceIdType.MESH
BF = jnp.bfloat16
F32 = jnp.float32

SCALE_T = math.log2(math.e) / math.sqrt(TREL)
SCALE_S = math.log2(math.e) / math.sqrt(SREL)
OFFSET = 60.0


def params(mesh):
    return mesh.shape["seq"], mesh.shape["head"]


ORDER = (1, 3, 2, 0)
EARLY = 2


def xor2(a, b):
    bits = [lax.rem(lax.div(a, w) + lax.div(b, w), 2) * w for w in (1, 2)]
    return bits[0] + bits[1]


def kernel(
    seq_n, head_n, rows, chunk,
    kept_ref, teach_hbm, stud_hbm, out_ref,
    teach_in, stud_in, stud_out, packed, tea, stu, tea_shift, stu_query, sums, rows_out, rows_in,
    in_t, in_sem, send_t, send_s, recv_t, recv_s, send_o, recv_o,
):
    total = seq_n * head_n
    seq_me = lax.axis_index("seq")
    head_me = lax.axis_index("head")
    me = seq_me * head_n + head_me
    positions = rows * total
    chunks = positions // chunk
    per_chunk = chunk // rows
    my_chunk = lax.div(seq_me, 4)
    core_me = lax.rem(head_me, 2)
    y_me = lax.div(head_me, 2)
    x_me = lax.rem(seq_me, 4)

    def chunk_at(step, core):
        code = jnp.int32(ORDER[0])
        for i in range(1, chunks):
            code = jnp.where(step == i, ORDER[i], code)
        return xor2(xor2(my_chunk, code), 2 * core)

    barrier = pltpu.get_barrier_semaphore()

    heads_from_me = [lax.rem(head_me + i, head_n) for i in range(head_n)]
    for h in heads_from_me[1:]:
        pl.semaphore_signal(barrier, inc=1, device_id=(seq_me, h), device_id_type=MESH)

    @pl.loop(1, seq_n)
    def _(k):
        s = lax.rem(seq_me + k, seq_n)
        for h in heads_from_me:
            pl.semaphore_signal(barrier, inc=1, device_id=(s, h), device_id_type=MESH)

    load_t = pltpu.make_async_copy(teach_hbm, teach_in, in_t)
    load_t.start()

    @pl.loop(0, HEADS)
    def _(i):
        head = stud_hbm.at[:, :, pl.ds(pl.multiple_of(i * HD, HD), HD)]
        pltpu.make_async_copy(head, stud_in.at[i], in_sem).start()

    load_t.wait()
    pl.semaphore_wait(barrier, total - 1)

    mine = pl.ds(pl.multiple_of(me * rows, rows), rows)

    def teach_src(s, h):
        r = h * 8 + lax.rem(s, 8)
        return teach_in.at[lax.div(s, 8), :, pl.ds(pl.multiple_of(r * TREL, TREL), TREL)]

    own_t = pltpu.make_async_copy(teach_src(seq_me, head_me), tea.at[mine], recv_t.at[my_chunk])
    own_s = pltpu.make_async_copy(stud_out.at[me], packed.at[me], recv_s.at[my_chunk])
    own_t.start()

    x_at = [lax.rem(x_me + i, 4) for i in range(4)]
    y_at = [lax.rem(y_me + i, 4) for i in range(4)]

    def send_teach(s, h):
        pltpu.make_async_remote_copy(
            src_ref=teach_src(s, h), dst_ref=tea.at[mine], send_sem=send_t, recv_sem=recv_t.at[my_chunk],
            device_id=(s, h), device_id_type=MESH,
        ).start()

    def send_stud(s, h):
        pltpu.make_async_remote_copy(
            src_ref=stud_out.at[s * head_n + h], dst_ref=packed.at[me], send_sem=send_s,
            recv_sem=recv_s.at[my_chunk], device_id=(s, h), device_id_type=MESH,
        ).start()

    def send(step, *kinds):
        chunk_of = [chunk_at(step, core) for core in range(2)]
        for j in range(per_chunk):
            core, x = j % 2, (j // 2) % 4
            y = (x + j // 8) % 4
            s = chunk_of[core] * 4 + x_at[x]
            h = y_at[y] * 2 + core

            def copies(s=s, h=h):
                for kind in kinds:
                    kind(s, h)

            if x == 0 and y == 0:
                pl.when((s != seq_me) | (h != head_me))(copies)
            else:
                copies()

    @pl.loop(0, EARLY)
    def _(step):
        send(step, send_teach)

    pltpu.make_async_copy(stud_in, stud_in, in_sem).wait()

    lane = lax.broadcasted_iota(jnp.int32, (rows, HD), 1)
    tile_lane = lax.broadcasted_iota(jnp.int32, (8, HD), 1)

    @pl.loop(0, 2 * head_n)
    def _(bg):
        b = lax.div(bg, head_n)
        g = lax.rem(bg, head_n)
        heads = [stud_in[kept_ref[5 * g + i], b].astype(F32) for i in range(5)]
        for u in range(8):
            first = (u * SREL) // HD
            offset = (u * SREL) % HD
            piece = heads[first]
            if offset:
                piece = pltpu.roll(piece, HD - offset, 1)
            if offset + SREL > HD:
                other = pltpu.roll(heads[first + 1], HD - offset, 1)
                piece = jnp.where(lane < HD - offset, piece, other)
            v = piece.reshape(4, 8, HD)
            rest = [pltpu.roll(v[i], 64 + 16 * i, 1) for i in range(4)]
            rest = jnp.where(tile_lane < 32, jnp.where(tile_lane < 16, rest[0], rest[1]), jnp.where(tile_lane < 48, rest[2], rest[3]))
            to = (b * 8 + u) * head_n + g
            stud_out[to, 0] = jnp.where(tile_lane < 64, v[0], pltpu.roll(v[2], 64, 1)).astype(BF)
            stud_out[to, 1] = jnp.where(tile_lane < 64, v[1], pltpu.roll(v[3], 64, 1)).astype(BF)
            stud_out[to, 2] = rest.astype(BF)

    own_s.start()

    @pl.loop(0, EARLY)
    def _(step):
        send(step, send_stud)

    @pl.loop(EARLY, chunks)
    def _(step):
        send(step, send_teach, send_stud)

    sums[...] = jnp.zeros_like(sums)
    part = 256
    row_i = lax.broadcasted_iota(jnp.int32, (TREL, HD), 0)
    col_i = lax.broadcasted_iota(jnp.int32, (TREL, HD), 1)
    pick_t = jnp.where(col_i == 0, 1.0, 0.0).astype(BF)
    pick_s = jnp.where((col_i == SREL) & (row_i < SREL), 1.0, 0.0).astype(BF)
    chunk_lane = lax.broadcasted_iota(jnp.int32, (chunk, HD), 1)
    ones_t = jnp.where(chunk_lane == 0, 1.0, 0.0).astype(BF)

    def rows_dot(x, y):
        return lax.dot_general(x, y, (((1,), (1,)), ((), ())), preferred_element_type=F32)

    def scores(key_start, key_count, query_start):
        keys = pl.ds(pl.multiple_of(key_start, part), key_count)
        queries = pl.ds(pl.multiple_of(query_start, part), part)
        key_t = jnp.concatenate([tea[keys], ones_t[:key_count]], axis=1)
        key_s = stu[keys]
        key_s = jnp.concatenate([key_s, key_s], axis=1)
        query_t = jnp.concatenate([tea[queries], tea_shift[queries]], axis=1)
        return rows_dot(key_t, query_t) * SCALE_T, rows_dot(key_s, stu_query[queries])

    def add(query_start, pairs):
        queries = pl.ds(pl.multiple_of(query_start, part), part)
        fold = lambda x: jnp.sum(x.reshape(-1, 8, part), axis=0)
        for score_t, score_s in pairs:
            weight_t = jnp.exp2(score_t)
            weight_s = jnp.exp2(score_s)
            sums[0, :, queries] += fold(weight_t)
            sums[1, :, queries] += fold(weight_s)
            sums[2, :, queries] += fold(weight_t * (score_t - score_s))

    def below(key_start, query_start):
        for q in range(0, chunk, part):
            add(query_start + q, [scores(key_start, chunk, query_start + q)])

    def diagonal(start):
        key_i = lax.broadcasted_iota(jnp.int32, (part, part), 0)
        query_i = lax.broadcasted_iota(jnp.int32, (part, part), 1)
        seen = key_i <= query_i
        for q in range(0, chunk, part):
            score_t, score_s = scores(start, q + part, start + q)
            pairs = [(jnp.where(seen, score_t[q:], -1e30), jnp.where(seen, score_s[q:], -1e30))]
            if q:
                pairs.append((score_t[:q], score_s[:q]))
            add(start + q, pairs)

    @pl.loop(0, chunks)
    def _(n):
        c = chunk_at(n, core_me)
        here = pl.ds(pl.multiple_of(c * chunk, chunk), chunk)
        pltpu.make_async_copy(tea.at[here], tea.at[here], recv_t.at[c]).wait()
        from_c = pl.ds(pl.multiple_of(c * per_chunk, per_chunk), per_chunk)
        pltpu.make_async_copy(packed.at[from_c], packed.at[from_c], recv_s.at[c]).wait()

        a = tea[here].astype(F32)
        norm_t = jnp.dot((a * a).astype(BF), pick_t, preferred_element_type=F32)
        tea_shift[here] = jnp.where(chunk_lane == 0, -OFFSET / SCALE_T - norm_t, 0.0).astype(BF)
        u = packed[from_c].astype(F32)
        lanes = lax.broadcasted_iota(jnp.int32, (per_chunk, 8, HD), 2)
        first = [u[:, 0], u[:, 1], pltpu.roll(u[:, 0], 64, 2), pltpu.roll(u[:, 1], 64, 2)]
        b = jnp.stack(
            [jnp.where(lanes < 64, first[i], pltpu.roll(u[:, 2], 64 - 16 * i, 2)) for i in range(4)], axis=1
        ).reshape(chunk, HD)
        b = jnp.where(chunk_lane < SREL, b, 0.0)
        stu[here] = jnp.where(chunk_lane == SREL, 1.0, b).astype(BF)
        norm_s = jnp.dot((b * b).astype(BF), pick_s, preferred_element_type=F32)
        scaled = b * SCALE_S
        high = scaled.astype(BF)
        low = (scaled - high.astype(F32)).astype(BF)
        high = jnp.where(chunk_lane == SREL, -OFFSET - SCALE_S * norm_s, high.astype(F32)).astype(BF)
        stu_query[here] = jnp.concatenate([high, low], axis=1)

        @pl.loop(0, n)
        def _(m):
            d = chunk_at(m, core_me)
            upper, lower = jnp.maximum(c, d), jnp.minimum(c, d)
            below(lower * chunk, upper * chunk)

        diagonal(c * chunk)

    each = positions // seq_n
    for k in range(1, seq_n + 1):
        to = lax.rem(seq_me + k, seq_n)
        part = pl.ds(pl.multiple_of(to * each, each), each)
        total_t = jnp.sum(sums[0, :, part], axis=0, keepdims=True)
        total_s = jnp.sum(sums[1, :, part], axis=0, keepdims=True)
        cross = jnp.sum(sums[2, :, part], axis=0, keepdims=True)
        rows_out[to] = (cross / total_t - jnp.log2(total_t) + jnp.log2(total_s)) * math.log(2.0)
        if k < seq_n:
            pltpu.make_async_remote_copy(
                src_ref=rows_out.at[to], dst_ref=rows_in.at[seq_me], send_sem=send_o, recv_sem=recv_o,
                device_id=(to, head_me), device_id_type=MESH,
            ).start()
        else:
            pltpu.make_async_copy(rows_out.at[to], rows_in.at[to], recv_o).start()

    pltpu.make_async_copy(rows_in, rows_in, recv_o).wait()
    out_ref[...] = rows_in[...].reshape(2, 8, each)

    sent = pl.ds(0, (total - 1) * rows)
    sent_s = pl.ds(0, total - 1)
    pltpu.make_async_copy(tea.at[sent], tea.at[sent], send_t).wait()
    pltpu.make_async_copy(packed.at[sent_s], packed.at[sent_s], send_s).wait()
    others = pl.ds(0, seq_n - 1)
    pltpu.make_async_copy(rows_in.at[others], rows_in.at[others], send_o).wait()


def shards(seq_n, head_n, teacher_query, student_query, kept_heads):
    batch, rows, width = teacher_query.shape
    total = seq_n * head_n
    positions = rows * total
    chunk = 1024
    chunks = positions // chunk
    each = positions // seq_n
    vm = pltpu.VMEM
    dma = pltpu.SemaphoreType.DMA
    return pl.pallas_call(
        functools.partial(kernel, seq_n, head_n, rows, chunk),
        out_shape=jax.ShapeDtypeStruct((batch, RELH // head_n, each), F32),
        in_specs=[
            pl.BlockSpec(memory_space=pltpu.SMEM),
            pl.BlockSpec(memory_space=pltpu.HBM),
            pl.BlockSpec(memory_space=pltpu.HBM),
        ],
        out_specs=pl.BlockSpec(memory_space=pltpu.VMEM),
        scratch_shapes=[
            vm((batch, rows, width), BF),
            vm((HEADS, batch, rows, HD), BF),
            vm((total, 3, 8, HD), BF),
            vm((total, 3, 8, HD), BF),
            vm((positions, TREL), BF),
            vm((positions, HD), BF),
            vm((positions, HD), BF),
            vm((positions, 2 * HD), BF),
            vm((3, 8, positions), F32),
            vm((seq_n, 1, each), F32),
            vm((seq_n, 1, each), F32),
            dma, dma, dma, dma, dma((chunks,)), dma((chunks,)), dma, dma,
        ],
        compiler_params=pltpu.CompilerParams(
            collective_id=0, has_side_effects=True, vmem_limit_bytes=60 * 2**20
        ),
    )(kept_heads, teacher_query, student_query)


def solution(mesh):
    seq_n, head_n = params(mesh)
    placed = (P(None, ("seq", "head"), None), P(None, ("seq", "head"), None), P())
    return jax.shard_map(
        functools.partial(shards, seq_n, head_n),
        mesh=mesh, in_specs=placed, out_specs=P(None, "head", "seq"), check_vma=False,
    )
```

```python
import functools
import math

import jax
import jax.numpy as jnp
from jax import lax
from jax.experimental import pallas as pl
from jax.experimental.pallas import tpu as pltpu
from jax.sharding import PartitionSpec as P

HEADS = 64
HD = 128
KEPT = 40
RELH = 64
TREL = 128
SREL = 80

MESH = pl.DeviceIdType.MESH
BF = jnp.bfloat16
F32 = jnp.float32

SCALE_T = math.log2(math.e) / math.sqrt(TREL)
SCALE_S = math.log2(math.e) / math.sqrt(SREL)
OFFSET = 60.0


def params(mesh):
    return mesh.shape["seq"], mesh.shape["head"]


ORDER = (1, 3, 2, 0)
EARLY = 3


def xor2(a, b):
    bits = [lax.rem(lax.div(a, w) + lax.div(b, w), 2) * w for w in (1, 2)]
    return bits[0] + bits[1]


def kernel(
    seq_n, head_n, rows, chunk,
    kept_ref, teach_hbm, stud_hbm, out_ref,
    teach_in, stud_in, stud_out, packed, tea, stu, tea_shift, stu_query, sums, rows_out, rows_in,
    in_t, in_sem, send_t, send_s, recv_t, recv_s, send_o, recv_o,
):
    total = seq_n * head_n
    seq_me = lax.axis_index("seq")
    head_me = lax.axis_index("head")
    me = seq_me * head_n + head_me
    positions = rows * total
    chunks = positions // chunk
    per_chunk = chunk // rows
    my_chunk = lax.div(seq_me, 4)
    core_me = lax.rem(head_me, 2)
    y_me = lax.div(head_me, 2)
    x_me = lax.rem(seq_me, 4)

    def chunk_at(step, core):
        code = jnp.int32(ORDER[0])
        for i in range(1, chunks):
            code = jnp.where(step == i, ORDER[i], code)
        return xor2(xor2(my_chunk, code), 2 * core)

    load_t = pltpu.make_async_copy(teach_hbm, teach_in, in_t)
    load_t.start()

    barrier = pltpu.get_barrier_semaphore()

    heads_from_me = [lax.rem(head_me + i, head_n) for i in range(head_n)]
    for h in heads_from_me[1:]:
        pl.semaphore_signal(barrier, inc=1, device_id=(seq_me, h), device_id_type=MESH)

    @pl.loop(1, seq_n)
    def _(k):
        s = lax.rem(seq_me + k, seq_n)
        for h in heads_from_me:
            pl.semaphore_signal(barrier, inc=1, device_id=(s, h), device_id_type=MESH)

    @pl.loop(0, HEADS)
    def _(i):
        head = stud_hbm.at[:, :, pl.ds(pl.multiple_of(i * HD, HD), HD)]
        pltpu.make_async_copy(head, stud_in.at[i], in_sem).start()

    load_t.wait()
    pl.semaphore_wait(barrier, total - 1)

    mine = pl.ds(pl.multiple_of(me * rows, rows), rows)

    def teach_src(s, h):
        r = h * 8 + lax.rem(s, 8)
        return teach_in.at[lax.div(s, 8), :, pl.ds(pl.multiple_of(r * TREL, TREL), TREL)]

    own_t = pltpu.make_async_copy(teach_src(seq_me, head_me), tea.at[mine], recv_t.at[my_chunk])
    own_s = pltpu.make_async_copy(stud_out.at[me], packed.at[me], recv_s.at[my_chunk])
    own_t.start()

    x_at = [lax.rem(x_me + i, 4) for i in range(4)]
    y_at = [lax.rem(y_me + i, 4) for i in range(4)]

    def send_teach(s, h):
        pltpu.make_async_remote_copy(
            src_ref=teach_src(s, h), dst_ref=tea.at[mine], send_sem=send_t, recv_sem=recv_t.at[my_chunk],
            device_id=(s, h), device_id_type=MESH,
        ).start()

    def send_stud(s, h):
        pltpu.make_async_remote_copy(
            src_ref=stud_out.at[s * head_n + h], dst_ref=packed.at[me], send_sem=send_s,
            recv_sem=recv_s.at[my_chunk], device_id=(s, h), device_id_type=MESH,
        ).start()

    def send(step, *kinds):
        chunk_of = [chunk_at(step, core) for core in range(2)]
        for j in range(per_chunk):
            core, x = j % 2, (1, 3, 2, 0)[(j // 2 + 2 * (j % 2)) % 4]
            y = (x + (3, 1, 2, 0)[j // 8]) % 4
            s = chunk_of[core] * 4 + x_at[x]
            h = y_at[y] * 2 + core

            def copies(s=s, h=h):
                for kind in kinds:
                    kind(s, h)

            if x == 0 and y == 0:
                pl.when((s != seq_me) | (h != head_me))(copies)
            else:
                copies()

    @pl.loop(0, EARLY)
    def _(step):
        send(step, send_teach)

    pltpu.make_async_copy(stud_in, stud_in, in_sem).wait()

    lane = lax.broadcasted_iota(jnp.int32, (rows, HD), 1)
    tile_lane = lax.broadcasted_iota(jnp.int32, (8, HD), 1)

    @pl.loop(0, 2 * head_n)
    def _(bg):
        b = lax.div(bg, head_n)
        g = lax.rem(bg, head_n)
        heads = [stud_in[kept_ref[5 * g + i], b].astype(F32) for i in range(5)]
        for u in range(8):
            first = (u * SREL) // HD
            offset = (u * SREL) % HD
            piece = heads[first]
            if offset:
                piece = pltpu.roll(piece, HD - offset, 1)
            if offset + SREL > HD:
                other = pltpu.roll(heads[first + 1], HD - offset, 1)
                piece = jnp.where(lane < HD - offset, piece, other)
            v = piece.reshape(4, 8, HD)
            rest = [pltpu.roll(v[i], 64 + 16 * i, 1) for i in range(4)]
            rest = jnp.where(tile_lane < 32, jnp.where(tile_lane < 16, rest[0], rest[1]), jnp.where(tile_lane < 48, rest[2], rest[3]))
            to = (b * 8 + u) * head_n + g
            stud_out[to, 0] = jnp.where(tile_lane < 64, v[0], pltpu.roll(v[2], 64, 1)).astype(BF)
            stud_out[to, 1] = jnp.where(tile_lane < 64, v[1], pltpu.roll(v[3], 64, 1)).astype(BF)
            stud_out[to, 2] = rest.astype(BF)

    own_s.start()

    @pl.loop(0, EARLY)
    def _(step):
        send(step, send_stud)

    @pl.loop(EARLY, chunks)
    def _(step):
        send(step, send_teach, send_stud)

    sums[...] = jnp.zeros_like(sums)
    part = 256
    row_i = lax.broadcasted_iota(jnp.int32, (TREL, HD), 0)
    col_i = lax.broadcasted_iota(jnp.int32, (TREL, HD), 1)
    pick_t = jnp.where(col_i == 0, 1.0, 0.0).astype(BF)
    pick_s = jnp.where((col_i == SREL) & (row_i < SREL), 1.0, 0.0).astype(BF)
    chunk_lane = lax.broadcasted_iota(jnp.int32, (chunk, HD), 1)
    ones_t = jnp.where(chunk_lane == 0, 1.0, 0.0).astype(BF)

    def rows_dot(x, y):
        return lax.dot_general(x, y, (((1,), (1,)), ((), ())), preferred_element_type=F32)

    def scores(key_start, key_count, query_start):
        keys = pl.ds(pl.multiple_of(key_start, part), key_count)
        queries = pl.ds(pl.multiple_of(query_start, part), part)
        key_t = jnp.concatenate([tea[keys], ones_t[:key_count]], axis=1)
        key_s = stu[keys]
        key_s = jnp.concatenate([key_s, key_s], axis=1)
        query_t = jnp.concatenate([tea[queries], tea_shift[queries]], axis=1)
        return rows_dot(key_t, query_t) * SCALE_T, rows_dot(key_s, stu_query[queries])

    def add(query_start, pairs):
        queries = pl.ds(pl.multiple_of(query_start, part), part)
        fold = lambda x: jnp.sum(x.reshape(-1, 8, part), axis=0)
        for score_t, score_s in pairs:
            weight_t = jnp.exp2(score_t)
            weight_s = jnp.exp2(score_s)
            sums[0, :, queries] += fold(weight_t)
            sums[1, :, queries] += fold(weight_s)
            sums[2, :, queries] += fold(weight_t * (score_t - score_s))

    def below(key_start, query_start):
        for q in range(0, chunk, part):
            add(query_start + q, [scores(key_start, chunk, query_start + q)])

    def diagonal(start):
        key_i = lax.broadcasted_iota(jnp.int32, (part, part), 0)
        query_i = lax.broadcasted_iota(jnp.int32, (part, part), 1)
        seen = key_i <= query_i
        for q in range(0, chunk, part):
            score_t, score_s = scores(start, q + part, start + q)
            pairs = [(jnp.where(seen, score_t[q:], -1e30), jnp.where(seen, score_s[q:], -1e30))]
            if q:
                pairs.append((score_t[:q], score_s[:q]))
            add(start + q, pairs)

    @pl.loop(0, chunks)
    def _(n):
        c = chunk_at(n, core_me)
        here = pl.ds(pl.multiple_of(c * chunk, chunk), chunk)
        pltpu.make_async_copy(tea.at[here], tea.at[here], recv_t.at[c]).wait()
        from_c = pl.ds(pl.multiple_of(c * per_chunk, per_chunk), per_chunk)
        pltpu.make_async_copy(packed.at[from_c], packed.at[from_c], recv_s.at[c]).wait()

        a = tea[here].astype(F32)
        norm_t = jnp.dot((a * a).astype(BF), pick_t, preferred_element_type=F32)
        tea_shift[here] = jnp.where(chunk_lane == 0, -OFFSET / SCALE_T - norm_t, 0.0).astype(BF)
        u = packed[from_c].astype(F32)
        lanes = lax.broadcasted_iota(jnp.int32, (per_chunk, 8, HD), 2)
        first = [u[:, 0], u[:, 1], pltpu.roll(u[:, 0], 64, 2), pltpu.roll(u[:, 1], 64, 2)]
        b = jnp.stack(
            [jnp.where(lanes < 64, first[i], pltpu.roll(u[:, 2], 64 - 16 * i, 2)) for i in range(4)], axis=1
        ).reshape(chunk, HD)
        b = jnp.where(chunk_lane < SREL, b, 0.0)
        stu[here] = jnp.where(chunk_lane == SREL, 1.0, b).astype(BF)
        norm_s = jnp.dot((b * b).astype(BF), pick_s, preferred_element_type=F32)
        scaled = b * SCALE_S
        high = scaled.astype(BF)
        low = (scaled - high.astype(F32)).astype(BF)
        high = jnp.where(chunk_lane == SREL, -OFFSET - SCALE_S * norm_s, high.astype(F32)).astype(BF)
        stu_query[here] = jnp.concatenate([high, low], axis=1)

        @pl.loop(0, n)
        def _(m):
            d = chunk_at(m, core_me)
            upper, lower = jnp.maximum(c, d), jnp.minimum(c, d)
            below(lower * chunk, upper * chunk)

        diagonal(c * chunk)

    each = positions // seq_n
    for k in range(1, seq_n + 1):
        to = lax.rem(seq_me + k, seq_n)
        part = pl.ds(pl.multiple_of(to * each, each), each)
        total_t = jnp.sum(sums[0, :, part], axis=0, keepdims=True)
        total_s = jnp.sum(sums[1, :, part], axis=0, keepdims=True)
        cross = jnp.sum(sums[2, :, part], axis=0, keepdims=True)
        rows_out[to] = (cross / total_t - jnp.log2(total_t) + jnp.log2(total_s)) * math.log(2.0)
        if k < seq_n:
            pltpu.make_async_remote_copy(
                src_ref=rows_out.at[to], dst_ref=rows_in.at[seq_me], send_sem=send_o, recv_sem=recv_o,
                device_id=(to, head_me), device_id_type=MESH,
            ).start()
        else:
            pltpu.make_async_copy(rows_out.at[to], rows_in.at[to], recv_o).start()

    pltpu.make_async_copy(rows_in, rows_in, recv_o).wait()
    out_ref[...] = rows_in[...].reshape(2, 8, each)

    sent = pl.ds(0, (total - 1) * rows)
    sent_s = pl.ds(0, total - 1)
    pltpu.make_async_copy(tea.at[sent], tea.at[sent], send_t).wait()
    pltpu.make_async_copy(packed.at[sent_s], packed.at[sent_s], send_s).wait()
    others = pl.ds(0, seq_n - 1)
    pltpu.make_async_copy(rows_in.at[others], rows_in.at[others], send_o).wait()


def shards(seq_n, head_n, teacher_query, student_query, kept_heads):
    batch, rows, width = teacher_query.shape
    total = seq_n * head_n
    positions = rows * total
    chunk = 1024
    chunks = positions // chunk
    each = positions // seq_n
    vm = pltpu.VMEM
    dma = pltpu.SemaphoreType.DMA
    return pl.pallas_call(
        functools.partial(kernel, seq_n, head_n, rows, chunk),
        out_shape=jax.ShapeDtypeStruct((batch, RELH // head_n, each), F32),
        in_specs=[
            pl.BlockSpec(memory_space=pltpu.SMEM),
            pl.BlockSpec(memory_space=pltpu.HBM),
            pl.BlockSpec(memory_space=pltpu.HBM),
        ],
        out_specs=pl.BlockSpec(memory_space=pltpu.VMEM),
        scratch_shapes=[
            vm((batch, rows, width), BF),
            vm((HEADS, batch, rows, HD), BF),
            vm((total, 3, 8, HD), BF),
            vm((total, 3, 8, HD), BF),
            vm((positions, TREL), BF),
            vm((positions, HD), BF),
            vm((positions, HD), BF),
            vm((positions, 2 * HD), BF),
            vm((3, 8, positions), F32),
            vm((seq_n, 1, each), F32),
            vm((seq_n, 1, each), F32),
            dma, dma, dma, dma, dma((chunks,)), dma((chunks,)), dma, dma,
        ],
        compiler_params=pltpu.CompilerParams(
            collective_id=0, has_side_effects=True, vmem_limit_bytes=60 * 2**20
        ),
    )(kept_heads, teacher_query, student_query)


def solution(mesh):
    seq_n, head_n = params(mesh)
    placed = (P(None, ("seq", "head"), None), P(None, ("seq", "head"), None), P())
    return jax.shard_map(
        functools.partial(shards, seq_n, head_n),
        mesh=mesh, in_specs=placed, out_specs=P(None, "head", "seq"), check_vma=False,
    )
```
